32 devices in a mesh: ctx: 16 (over z, y, core), head: 2 (over x).
Axes of the slice: x: 2, y: 2, z: 4, core: 2. Of those that a mesh axis runs over, the one named last changes fastest.
Arguments:
- queries: bfloat16 [2048, 2048], P('ctx', 'head'), may hold values from -8 to 8, as said below
- key_codes: bfloat16 [2, 2048, 128], P(None, 'ctx'), may hold values from -6 to 6
- key_scale: float32 [2, 2048], P(None, 'ctx'), may hold values from 0.5 to 2
- value_codes: bfloat16 [2, 2048, 128], P(None, 'ctx'), may hold values from -6 to 6
- value_scale: float32 [2, 2048], P(None, 'ctx'), may hold values from 0.5 to 2
- evict_flags: int32 [2, 2048], P(None, 'ctx'), may hold values from 0 to 1, as said below
- out_forward: bfloat16 [2048, 2048], P('ctx', 'head'), may hold values from -12 to 12, as said below
- grad_output: bfloat16 [2048, 2048], P('ctx', 'head'), may hold values from -6 to 6
- log_norm: float32 [16, 2048], P('head', 'ctx'), as said below
Outputs:
- grad_queries: bfloat16 [2048, 2048], P('ctx', 'head')
- grad_keys: bfloat16 [2, 2048, 128], P(None, 'ctx')
- grad_values: bfloat16 [2, 2048, 128], P(None, 'ctx')
The draws below stay inside these ranges and needn't reach their ends.
Inputs may be any that keep to these rules, and one draw needn't show every extreme that they name: queries hold bfloat16 values. `evict_flags`: each token and key and value head is evicted independently with probability one half. log_norm is the log of the sum of exp(c * scores) over the visible keys of each query, from the same queries, keys and flags. out_forward is the forward attention output of the same inputs, rounded to bfloat16.
All inputs are finite; a program needn't handle non-finite values.
Results may differ from the reference program's by a relative error of at most 0.0033.
The reference program's roundings to bfloat16 on the way count: a program that leaves them out, or rounds other values in their place, can miss the bound.
Values may be sent and summed in bfloat16 or wider, within the bound.
A program may use at most 64 MiB of HBM per device.

```python
import math
import jax
import jax.numpy as jnp
from jax import lax

CHANNEL_DIM = 128
ASKER_PROJ_NUM = 16
KEY_VALUE_HEADS = 2
TOK_DEV = 128
SEQUENCE_TOKENS = 2048
DELAY = 256


def token_position_drawn(rows, tok_dev, ctx_count):
    device_row = rows // tok_dev
    within = rows % tok_dev
    half = tok_dev // 2
    return jnp.where(within < half, device_row * half + within, (2 * ctx_count - 1 - device_row) * half + within - half).astype(jnp.int32)


def base_inputs(key):
    queries = jax.random.normal(jax.random.fold_in(key, 101), (SEQUENCE_TOKENS, ASKER_PROJ_NUM * CHANNEL_DIM), jnp.float32)
    value_codes = jnp.clip(jax.random.normal(jax.random.fold_in(key, 103), (KEY_VALUE_HEADS, SEQUENCE_TOKENS, CHANNEL_DIM), jnp.float32), -6.0, 6.0)
    queries = jnp.clip(queries, -6.0, 6.0)
    key_codes = jnp.clip(jax.random.normal(jax.random.fold_in(key, 102), (KEY_VALUE_HEADS, SEQUENCE_TOKENS, CHANNEL_DIM), jnp.float32), -6.0, 6.0)
    key_scale = jnp.exp(jax.random.uniform(jax.random.fold_in(key, 105), (KEY_VALUE_HEADS, SEQUENCE_TOKENS), jnp.float32, math.log(0.5), math.log(2.0)))
    value_scale = jnp.exp(jax.random.uniform(jax.random.fold_in(key, 106), (KEY_VALUE_HEADS, SEQUENCE_TOKENS), jnp.float32, math.log(0.5), math.log(2.0)))
    evict_flags = jax.random.randint(jax.random.fold_in(key, 107), (KEY_VALUE_HEADS, SEQUENCE_TOKENS), 0, 2, dtype=jnp.int32)
    return (queries.astype(jnp.bfloat16), key_codes.astype(jnp.bfloat16), key_scale, value_codes.astype(jnp.bfloat16), value_scale, evict_flags)


def forward_outputs(key):
    queries, key_codes, key_scale, value_codes, value_scale, evict_flags = base_inputs(key)
    group_width = ASKER_PROJ_NUM // KEY_VALUE_HEADS
    softmax_factor = CHANNEL_DIM ** (-0.5)
    ctx_count = SEQUENCE_TOKENS // TOK_DEV
    key_deq = (key_codes.astype(jnp.float32) * key_scale[:, :, None]).astype(jnp.bfloat16).astype(jnp.float32)
    value_deq = (value_codes.astype(jnp.float32) * value_scale[:, :, None]).astype(jnp.bfloat16).astype(jnp.float32)
    lookup_entry_list = jnp.repeat(key_deq, group_width, axis=0)
    payload_entry_list = jnp.repeat(value_deq, group_width, axis=0)
    evict_all = jnp.repeat(evict_flags, group_width, axis=0)
    key_pos = token_position_drawn(jnp.arange(SEQUENCE_TOKENS, dtype=jnp.int32), TOK_DEV, ctx_count)
    tile_span = math.gcd(SEQUENCE_TOKENS, 256)
    query_float = queries.astype(jnp.float32)

    def one_block(offset):
        query_block_rows = lax.dynamic_slice_in_dim(query_float, offset, tile_span, 0).reshape(tile_span, ASKER_PROJ_NUM, CHANNEL_DIM)
        query_pos = token_position_drawn(offset + jnp.arange(tile_span, dtype=jnp.int32), TOK_DEV, ctx_count)
        score_matrix = jnp.einsum('aps,prs->par', query_block_rows, lookup_entry_list) * softmax_factor
        distance = query_pos[:, None] - key_pos[None, :]
        visible = (distance[None] >= 0) & ((evict_all[:, None, :] == 0) | (distance[None] < DELAY))
        score_matrix = jnp.where(visible, score_matrix, -jnp.inf)
        highest = jnp.max(score_matrix, axis=2)
        natural_powers = jnp.exp(score_matrix - highest[:, :, None])
        cumulative_sums = jnp.sum(natural_powers, axis=2)
        norm_blk = highest + jnp.log(cumulative_sums)
        result_lines = jnp.einsum('djt,dti->jdi', natural_powers, payload_entry_list) / cumulative_sums.T[:, :, None]
        return (norm_blk, result_lines.reshape(tile_span, ASKER_PROJ_NUM * CHANNEL_DIM))
    block_starts = jnp.arange(0, SEQUENCE_TOKENS, tile_span, dtype=jnp.int32)
    norms, result_lines = lax.map(one_block, block_starts)
    log_norm = jnp.transpose(norms, (1, 0, 2)).reshape(ASKER_PROJ_NUM, SEQUENCE_TOKENS)
    return (log_norm, result_lines.reshape(SEQUENCE_TOKENS, ASKER_PROJ_NUM * CHANNEL_DIM).astype(jnp.bfloat16))


def draw_queries(key, part):
    return base_inputs(key)[0]


def draw_key_codes(key, part):
    return base_inputs(key)[1]


def draw_key_scale(key, part):
    return base_inputs(key)[2]


def draw_value_codes(key, part):
    return base_inputs(key)[3]


def draw_value_scale(key, part):
    return base_inputs(key)[4]


def draw_evict_flags(key, part):
    return base_inputs(key)[5]


def draw_log_norm(key, part):
    return forward_outputs(key)[0]


def draw_out_forward(key, part):
    return forward_outputs(key)[1]


def shard_levels(key, shape, shards, least, high):
    level, own = 1.0, jax.random.fold_in(key, 6)
    for dim, shards_of in shards:
        steps = jnp.exp(jax.random.uniform(jax.random.fold_in(own, dim), (shards_of,), jnp.float32, least / len(shards), high / len(shards)))
        level = level * jnp.repeat(steps, shape[dim] // shards_of).reshape([-1 if axis == dim else 1 for axis in range(len(shape))])
    return level


def centred(rng, extent, scale, limit, pieces=(), held_as=jnp.bfloat16):
    entries = jax.random.normal(rng, extent, jnp.float32) * scale
    if len(pieces) > 0:
        entries = shard_levels(rng, extent, pieces, -0.22, 0.18) * entries
    return jnp.clip(entries, min=-limit, max=limit).astype(held_as)


def setup_inputs(seed: int = 0) -> dict:
    arg_keys = jax.random.split(jax.random.key(seed), 10)
    return {
        "queries": draw_queries(jax.random.fold_in(arg_keys[9], 71), 0),
        "key_codes": draw_key_codes(jax.random.fold_in(arg_keys[9], 71), 0),
        "key_scale": draw_key_scale(jax.random.fold_in(arg_keys[9], 71), 0),
        "value_codes": draw_value_codes(jax.random.fold_in(arg_keys[9], 71), 0),
        "value_scale": draw_value_scale(jax.random.fold_in(arg_keys[9], 71), 0),
        "evict_flags": draw_evict_flags(jax.random.fold_in(arg_keys[9], 71), 0),
        "out_forward": draw_out_forward(jax.random.fold_in(arg_keys[9], 71), 0),
        "grad_output": centred(arg_keys[7], (SEQUENCE_TOKENS, ASKER_PROJ_NUM * CHANNEL_DIM), 1.0, 6.0, ((0, 16), (1, 2))),
        "log_norm": draw_log_norm(jax.random.fold_in(arg_keys[9], 71), 0),
    }


def rounded(values):
    return lax.optimization_barrier(values.astype(jnp.bfloat16)).astype(jnp.float32)


def token_position(rows, tok_dev, ctx_count):
    device_row = rows // tok_dev
    within = rows % tok_dev
    half = tok_dev // 2
    return jnp.where(within < half, device_row * half + within, (2 * ctx_count - 1 - device_row) * half + within - half).astype(jnp.int32)


def reference(queries, key_codes, key_scale, value_codes, value_scale, evict_flags, out_forward, grad_output, log_norm):
    group_width = ASKER_PROJ_NUM // KEY_VALUE_HEADS
    softmax_factor = CHANNEL_DIM ** -0.5
    ctx_count = SEQUENCE_TOKENS // TOK_DEV
    key_deq = rounded(key_codes.astype(jnp.float32) * key_scale[:, :, None])
    value_deq = rounded(value_codes.astype(jnp.float32) * value_scale[:, :, None])
    lookup_entry_list = jnp.repeat(key_deq, group_width, axis=0)
    payload_entry_list = jnp.repeat(value_deq, group_width, axis=0)
    evict_all = jnp.repeat(evict_flags, group_width, axis=0)
    products = grad_output.astype(jnp.float32) * out_forward.astype(jnp.float32)
    row_delta = jnp.sum(products.reshape(SEQUENCE_TOKENS, ASKER_PROJ_NUM, CHANNEL_DIM), axis=2).T
    key_pos = token_position(jnp.arange(SEQUENCE_TOKENS, dtype=jnp.int32), TOK_DEV, ctx_count)
    tile_span = math.gcd(SEQUENCE_TOKENS, 256)

    def one_block(running, offset):
        key_total, value_total = running
        query_block_rows = lax.dynamic_slice_in_dim(queries, offset, tile_span, 0).astype(jnp.float32).reshape(tile_span, ASKER_PROJ_NUM, CHANNEL_DIM)
        gradient_block = lax.dynamic_slice_in_dim(grad_output, offset, tile_span, 0).astype(jnp.float32).reshape(tile_span, ASKER_PROJ_NUM, CHANNEL_DIM)
        norm_blk = lax.dynamic_slice_in_dim(log_norm, offset, tile_span, 1)
        delta_blk = lax.dynamic_slice_in_dim(row_delta, offset, tile_span, 1)
        query_pos = token_position(offset + jnp.arange(tile_span, dtype=jnp.int32), TOK_DEV, ctx_count)
        score_matrix = jnp.einsum("aps,prs->par", query_block_rows, lookup_entry_list) * softmax_factor
        distance = query_pos[:, None] - key_pos[None, :]
        visible = (distance[None] >= 0) & ((evict_all[:, None, :] == 0) | (distance[None] < DELAY))
        attention_weights = jnp.where(visible, jnp.exp(score_matrix - norm_blk[:, :, None]), 0.0)
        weight_gradient = jnp.einsum("aps,prs->par", gradient_block, payload_entry_list)
        score_gradient = softmax_factor * attention_weights * (weight_gradient - delta_blk[:, :, None])
        weight_block = rounded(attention_weights)
        logit_derivative_tile = rounded(score_gradient)
        asker_derivative = jnp.einsum("djt,dti->jdi", logit_derivative_tile, lookup_entry_list).reshape(tile_span, ASKER_PROJ_NUM * CHANNEL_DIM).astype(jnp.bfloat16)
        key_portion = jnp.einsum("jqs,qjx->jsx", logit_derivative_tile, query_block_rows).reshape(KEY_VALUE_HEADS, group_width, SEQUENCE_TOKENS, CHANNEL_DIM).sum(axis=1)
        value_portion = jnp.einsum("jqs,qjx->jsx", weight_block, gradient_block).reshape(KEY_VALUE_HEADS, group_width, SEQUENCE_TOKENS, CHANNEL_DIM).sum(axis=1)
        return (key_total + key_portion, value_total + value_portion), asker_derivative

    block_starts = jnp.arange(0, SEQUENCE_TOKENS, tile_span, dtype=jnp.int32)
    empty = jnp.zeros((KEY_VALUE_HEADS, SEQUENCE_TOKENS, CHANNEL_DIM), jnp.float32)
    (key_total, value_total), query_grads = lax.scan(one_block, (empty, empty), block_starts)
    return (query_grads.reshape(SEQUENCE_TOKENS, ASKER_PROJ_NUM * CHANNEL_DIM), key_total.astype(jnp.bfloat16), value_total.astype(jnp.bfloat16))
```

```python
import functools
import math

import jax
import jax.numpy as jnp
from jax import lax
from jax.experimental import pallas as pl
from jax.experimental.pallas import tpu as pltpu
from jax.sharding import PartitionSpec as P

ASKER_PROJ_NUM = 16
KEY_VALUE_HEADS = 2
DELAY = 256
FLAG_ROWS = 16
LOG2E = math.log2(math.e)
MESH = pl.DeviceIdType.MESH


def kernel(
    n,
    head_devices,
    q_ref,
    kc_ref,
    ks_ref,
    vc_ref,
    vs_ref,
    ev_ref,
    of_ref,
    go_ref,
    ln_ref,
    dq_ref,
    dk_ref,
    dv_ref,
    kv,
    part,
    core_in,
    y_in,
    z_in,
    q_rows,
    g_rows,
    q_cols,
    g_cols,
    norm,
    delta,
    dq_acc,
    group_sum,
    head_out,
    head_in,
    kz_send,
    kz_recv,
    ky_send,
    ky_recv,
    kc_send,
    kc_recv,
    rc_send,
    rc_recv,
    ry_send,
    ry_recv,
    rz_send,
    rz_recv,
    gs_send,
    gs_recv,
    h_send,
    h_recv,
):
    tokens, _ = q_ref.shape
    width = kc_ref.shape[2]
    heads = ln_ref.shape[0]
    half = tokens // 2
    zs = n // 4
    low_rows = 2 * half + FLAG_ROWS
    all_rows = 4 * half + FLAG_ROWS
    per_group = head_devices // KEY_VALUE_HEADS
    scale = width ** (-0.5)

    me = lax.axis_index("ctx")
    hd = lax.axis_index("head")
    c = lax.rem(me, 2)
    y = lax.rem(me // 2, 2)
    z = me // 4
    group = hd // per_group
    member = lax.rem(hd, per_group)

    def at(zi, yi, ci):
        return (zi * 4 + yi * 2 + ci, hd)

    core_peer = at(z, y, 1 - c)
    y_peer = at(z, 1 - y, c)
    other_group = (me, lax.rem(hd + per_group, head_devices))

    def turn(s):
        if zs & (zs - 1):
            return lax.rem(z + s, zs)
        out = 0
        bit = 1
        while bit < zs:
            out = out + lax.rem(z // bit + s // bit, 2) * bit
            bit *= 2
        return out

    barrier = pltpu.get_barrier_semaphore()
    pl.semaphore_signal(barrier, inc=1, device_id=core_peer, device_id_type=MESH)
    pl.semaphore_signal(barrier, inc=1, device_id=y_peer, device_id_type=MESH)
    pl.semaphore_signal(barrier, inc=1, device_id=other_group, device_id_type=MESH)
    for s in range(1, zs):
        pl.semaphore_signal(
            barrier, inc=1, device_id=at(turn(s), y, c), device_id_type=MESH
        )
    for s in range(1, per_group):
        pl.semaphore_signal(
            barrier,
            inc=1,
            device_id=(me, group * per_group + lax.rem(member + s, per_group)),
            device_id_type=MESH,
        )

    def column(row):
        return jnp.transpose(jnp.broadcast_to(row, (tokens, tokens)))

    key_col = column(ks_ref[pl.ds(group, 1), :])
    value_col = column(vs_ref[pl.ds(group, 1), :])
    keys = (kc_ref[group].astype(jnp.float32) * key_col).astype(jnp.bfloat16)
    values = (vc_ref[group].astype(jnp.float32) * value_col).astype(jnp.bfloat16)
    flags = ev_ref[pl.ds(group, 1), :].astype(jnp.float32)
    own = kv.at[z, y, c]
    own[0:half, :] = keys[0:half]
    own[half : 2 * half, :] = values[0:half]
    own[2 * half : low_rows, :] = jnp.broadcast_to(flags, (FLAG_ROWS, tokens)).astype(
        jnp.bfloat16
    )
    own[low_rows : low_rows + half, :] = keys[half:]
    own[low_rows + half :, :] = values[half:]

    pl.semaphore_wait(barrier, 3 + (zs - 1) + (per_group - 1))

    def sized(whole, f, full, low):
        @pl.when(whole)
        def _():
            f(pl.ds(0, full))

        @pl.when(jnp.logical_not(whole))
        def _():
            f(pl.ds(0, low))

    def kz_copy(src_z, dst_z, rows):
        return pltpu.make_async_remote_copy(
            src_ref=kv.at[z, y, c, rows],
            dst_ref=kv.at[src_z, y, c, rows],
            send_sem=kz_send.at[dst_z],
            recv_sem=kz_recv.at[src_z],
            device_id=at(dst_z, y, c),
            device_id_type=MESH,
        )

    def ky_copy(zi, yi, rows):
        ref = kv.at[zi, yi, c, rows]
        return pltpu.make_async_remote_copy(
            src_ref=ref,
            dst_ref=ref,
            send_sem=ky_send.at[zi],
            recv_sem=ky_recv.at[zi],
            device_id=y_peer,
            device_id_type=MESH,
        )

    def kc_copy(zi, ci, rows):
        ref = kv.at[zi, :, ci, rows]
        return pltpu.make_async_remote_copy(
            src_ref=ref,
            dst_ref=ref,
            send_sem=kc_send.at[zi],
            recv_sem=kc_recv.at[zi],
            device_id=core_peer,
            device_id_type=MESH,
        )

    def send_z(s, carry):
        zi = turn(s)
        sized(z >= zi, lambda rows: kz_copy(z, zi, rows).start(), all_rows, low_rows)
        return carry

    lax.fori_loop(1, zs, send_z, 0)

    def forward_y(s):
        zi = turn(s)

        def go(rows):
            @pl.when(zi != z)
            def _():
                kz_copy(zi, zi, rows).wait_recv()

            ky_copy(zi, y, rows).start()

        sized(zi >= z, go, all_rows, low_rows)

    def forward_c(s):
        zi = turn(s)

        def go(rows):
            ky_copy(zi, 1 - y, rows).wait_recv()
            kc_copy(zi, c, rows).start()

        sized(zi >= z, go, all_rows, low_rows)

    def ready(s):
        zi = turn(s)
        sized(
            zi >= z,
            lambda rows: kc_copy(zi, 1 - c, rows).wait_recv(),
            all_rows,
            low_rows,
        )

    forward_y(0)

    for side in range(2):
        tok = slice(side * half, (side + 1) * half)

        def by_head(ref):
            return jnp.concatenate(
                [ref[tok, h * width : (h + 1) * width] for h in range(heads)], axis=0
            )

        q = by_head(q_ref)
        g = by_head(go_ref)
        q_rows[side] = q
        g_rows[side] = g
        q_cols[side] = jnp.transpose(q)
        g_t = jnp.transpose(g)
        g_cols[side] = g_t
        o_t = jnp.transpose(by_head(of_ref))
        delta[side] = jnp.sum(
            g_t.astype(jnp.float32) * o_t.astype(jnp.float32), axis=0, keepdims=True
        )
        norm[side] = (
            jnp.concatenate([ln_ref[h : h + 1, tok] for h in range(heads)], axis=1)
            * LOG2E
        )
        dq_acc[side] = jnp.zeros(dq_acc.shape[1:], jnp.float32)

    chunk = 4 * half
    lanes = 2 * half
    copies = heads * half // lanes
    row = lax.broadcasted_iota(jnp.int32, (chunk, lanes), 0)
    lane = lax.broadcasted_iota(jnp.int32, (chunk, lanes), 1)
    row_block = row // half
    row_in = lax.rem(row, half)
    lane_in = lax.rem(lane, half)

    def terms(k, v, k_t, key_pos, limit, side):
        block = me if side == 0 else 2 * n - 1 - me
        distance = block * half + lane_in - key_pos
        visible = (distance >= 0) & (distance < limit)
        bias = jnp.where(visible, 0.0, -1e30)
        bias = jnp.concatenate([bias] * copies, axis=1)
        scores = jnp.dot(k, q_cols[side], preferred_element_type=jnp.float32)
        weights = jnp.exp2(scores * (scale * LOG2E) - norm[side] + bias)
        dweights = jnp.dot(v, g_cols[side], preferred_element_type=jnp.float32)
        dscores = (scale * weights * (dweights - delta[side])).astype(jnp.bfloat16)
        weights = weights.astype(jnp.bfloat16)
        dq_acc[side] += jnp.dot(k_t, dscores, preferred_element_type=jnp.float32)
        dk = jnp.dot(dscores, q_rows[side], preferred_element_type=jnp.float32)
        dv = jnp.dot(weights, g_rows[side], preferred_element_type=jnp.float32)
        return dk.reshape(2, 2, half, width), dv.reshape(2, 2, half, width)

    def limits(zi, first):
        cols = [
            column(kv[zi, yi, ci, 2 * half : 2 * half + FLAG_ROWS, :].astype(jnp.float32)[0:1])[
                first : first + half
            ]
            for yi in range(2)
            for ci in range(2)
        ]
        evicted = jnp.concatenate(cols, axis=0)
        return jnp.where(evicted == 0.0, 2 * n * half, DELAY)

    def compute(s):
        zi = turn(s)
        k = kv[zi, :, :, 0:half, :].reshape(chunk, width)
        v = kv[zi, :, :, half : 2 * half, :].reshape(chunk, width)
        k_t = jnp.transpose(k)
        key_pos = (zi * 4 + row_block) * half + row_in
        limit = limits(zi, 0)
        dk, dv = terms(k, v, k_t, key_pos, limit, 1)
        part[zi, :, :, 0:half, :] = dk
        part[zi, :, :, half : 2 * half, :] = dv

        @pl.when(zi <= z)
        def _():
            dk, dv = terms(k, v, k_t, key_pos, limit, 0)
            part[zi, :, :, 0:half, :] += dk
            part[zi, :, :, half : 2 * half, :] += dv

        @pl.when(zi >= z)
        def _():
            k = kv[zi, :, :, low_rows : low_rows + half, :].reshape(chunk, width)
            v = kv[zi, :, :, low_rows + half :, :].reshape(chunk, width)
            key_pos = (2 * n - 1 - zi * 4 - row_block) * half + row_in
            dk, dv = terms(k, v, jnp.transpose(k), key_pos, limits(zi, half), 1)
            part[zi, :, :, 2 * half : 3 * half, :] = dk
            part[zi, :, :, 3 * half :, :] = dv

    def rc_copy(zi, rows):
        return pltpu.make_async_remote_copy(
            src_ref=part.at[zi, :, 1 - c, rows],
            dst_ref=core_in.at[zi, :, rows],
            send_sem=rc_send.at[zi],
            recv_sem=rc_recv.at[zi],
            device_id=core_peer,
            device_id_type=MESH,
        )

    def ry_copy(zi, rows):
        return pltpu.make_async_remote_copy(
            src_ref=part.at[zi, 1 - y, c, rows],
            dst_ref=y_in.at[zi, rows],
            send_sem=ry_send.at[zi],
            recv_sem=ry_recv.at[zi],
            device_id=y_peer,
            device_id_type=MESH,
        )

    def rz_copy(src_z, dst_z, rows):
        return pltpu.make_async_remote_copy(
            src_ref=part.at[dst_z, y, c, rows],
            dst_ref=z_in.at[src_z, rows],
            send_sem=rz_send.at[dst_z],
            recv_sem=rz_recv.at[src_z],
            device_id=at(dst_z, y, c),
            device_id_type=MESH,
        )

    def reduce_c(s):
        zi = turn(s)
        sized(zi >= z, lambda rows: rc_copy(zi, rows).start(), 4 * half, 2 * half)

    def reduce_y(s):
        zi = turn(s)

        def go(rows):
            rc_copy(zi, rows).wait_recv()
            for yi in range(2):
                part[zi, yi, c, rows, :] += core_in[zi, yi, rows, :]
            ry_copy(zi, rows).start()

        sized(zi >= z, go, 4 * half, 2 * half)

    def reduce_z(s):
        zi = turn(s)

        def go(rows):
            ry_copy(zi, rows).wait_recv()
            part[zi, y, c, rows, :] += y_in[zi, rows, :]

            @pl.when(zi != z)
            def _():
                rz_copy(z, zi, rows).start()

        sized(zi >= z, go, 4 * half, 2 * half)

    def when(cond, f, s):
        @pl.when(cond)
        def _():
            f(s)

    forward_y(1)
    forward_c(0)

    def step(s, carry):
        when(s + 2 < zs, forward_y, s + 2)
        when(s + 1 < zs, forward_c, s + 1)
        ready(s)
        compute(s)
        reduce_c(s)
        when(s >= 1, reduce_y, s - 1)
        when(s >= 2, reduce_z, s - 2)
        return carry

    lax.fori_loop(0, zs, step, 0)
    reduce_y(zs - 1)
    if zs >= 2:
        reduce_z(zs - 2)
    reduce_z(zs - 1)

    for side in range(2):
        dq = jnp.transpose(dq_acc[side]).astype(jnp.bfloat16)
        for h in range(heads):
            dq_ref[side * half : (side + 1) * half, h * width : (h + 1) * width] = dq[
                h * half : (h + 1) * half
            ]

    def collect(s, carry):
        zi = turn(s)

        def go(rows):
            rz_copy(zi, zi, rows).wait_recv()
            part[z, y, c, rows, :] += z_in[zi, rows, :]

        sized(z >= zi, go, 4 * half, 2 * half)
        return carry

    lax.fori_loop(1, zs, collect, 0)

    total = part[z, y, c]
    if per_group > 1:
        group_sum[member] = total

        def gs_copy(src, s):
            return pltpu.make_async_remote_copy(
                src_ref=group_sum.at[member],
                dst_ref=group_sum.at[src],
                send_sem=gs_send.at[s],
                recv_sem=gs_recv.at[src],
                device_id=(me, group * per_group + lax.rem(member + s, per_group)),
                device_id_type=MESH,
            )

        for s in range(1, per_group):
            gs_copy(member, s).start()
        for s in range(1, per_group):
            gs_copy(lax.rem(member + s, per_group), s).wait_recv()
        for s in range(1, per_group):
            gs_copy(member, s).wait_send()
        total = group_sum[0]
        for s in range(1, per_group):
            total = total + group_sum[s]

    head_out[...] = total.astype(jnp.bfloat16)
    h_copy = pltpu.make_async_remote_copy(
        src_ref=head_out,
        dst_ref=head_in,
        send_sem=h_send,
        recv_sem=h_recv,
        device_id=other_group,
        device_id_type=MESH,
    )
    h_copy.start()

    def put(index, block):
        dk_ref[index, 0:half, :] = block[0:half, :]
        dv_ref[index, 0:half, :] = block[half : 2 * half, :]
        dk_ref[index, half:, :] = block[2 * half : 3 * half, :]
        dv_ref[index, half:, :] = block[3 * half :, :]

    put(group, head_out)

    def sent(s, carry):
        zi = turn(s)

        def own_z(rows):
            kz_copy(z, zi, rows).wait_send()

        def kept(rows):
            ky_copy(zi, y, rows).wait_send()
            kc_copy(zi, c, rows).wait_send()

        def summed(rows):
            rc_copy(zi, rows).wait_send()
            ry_copy(zi, rows).wait_send()

            @pl.when(zi != z)
            def _():
                rz_copy(z, zi, rows).wait_send()

        @pl.when(zi != z)
        def _():
            sized(z >= zi, own_z, all_rows, low_rows)

        sized(zi >= z, kept, all_rows, low_rows)
        sized(zi >= z, summed, 4 * half, 2 * half)
        return carry

    lax.fori_loop(0, zs, sent, 0)
    h_copy.wait()
    put(1 - group, head_in)


def local(
    queries,
    key_codes,
    key_scale,
    value_codes,
    value_scale,
    evict_flags,
    out_forward,
    grad_output,
    log_norm,
):
    n = lax.axis_size("ctx")
    head_devices = lax.axis_size("head")
    per_group = head_devices // KEY_VALUE_HEADS
    tokens = queries.shape[0]
    heads = log_norm.shape[0]
    width = key_codes.shape[2]
    half = tokens // 2
    zs = n // 4
    side_rows = heads * half
    f32, bf16 = jnp.float32, jnp.bfloat16
    vmem = pl.BlockSpec(memory_space=pltpu.VMEM)
    dma = pltpu.SemaphoreType.DMA
    return pl.pallas_call(
        functools.partial(kernel, n, head_devices),
        out_shape=(
            jax.ShapeDtypeStruct(queries.shape, bf16),
            jax.ShapeDtypeStruct(key_codes.shape, bf16),
            jax.ShapeDtypeStruct(value_codes.shape, bf16),
        ),
        in_specs=[vmem] * 9,
        out_specs=(vmem, vmem, vmem),
        scratch_shapes=[
            pltpu.VMEM((zs, 2, 2, 4 * half + FLAG_ROWS, width), bf16),
            pltpu.VMEM((zs, 2, 2, 4 * half, width), f32),
            pltpu.VMEM((zs, 2, 4 * half, width), f32),
            pltpu.VMEM((zs, 4 * half, width), f32),
            pltpu.VMEM((zs, 4 * half, width), f32),
            pltpu.VMEM((2, side_rows, width), bf16),
            pltpu.VMEM((2, side_rows, width), bf16),
            pltpu.VMEM((2, width, side_rows), bf16),
            pltpu.VMEM((2, width, side_rows), bf16),
            pltpu.VMEM((2, 1, side_rows), f32),
            pltpu.VMEM((2, 1, side_rows), f32),
            pltpu.VMEM((2, width, side_rows), f32),
            pltpu.VMEM((per_group, 4 * half, width), f32),
            pltpu.VMEM((4 * half, width), bf16),
            pltpu.VMEM((4 * half, width), bf16),
        ]
        + [dma((zs,))] * 12
        + [dma((per_group,))] * 2
        + [dma] * 2,
        compiler_params=pltpu.CompilerParams(
            collective_id=0, has_side_effects=True, vmem_limit_bytes=48 * 2**20
        ),
    )(
        queries,
        key_codes,
        key_scale,
        value_codes,
        value_scale,
        evict_flags,
        out_forward,
        grad_output,
        log_norm,
    )


def solution(mesh):
    in_specs = (
        P("ctx", "head"),
        P(None, "ctx", None),
        P(None, "ctx"),
        P(None, "ctx", None),
        P(None, "ctx"),
        P(None, "ctx"),
        P("ctx", "head"),
        P("ctx", "head"),
        P("head", "ctx"),
    )
    out_specs = (P("ctx", "head"), P(None, "ctx", None), P(None, "ctx", None))
    return jax.shard_map(local, mesh=mesh, in_specs=in_specs, out_specs=out_specs, check_vma=False)
```

```python
import functools
import math

import jax
import jax.numpy as jnp
from jax import lax
from jax.experimental import pallas as pl
from jax.experimental.pallas import tpu as pltpu
from jax.sharding import PartitionSpec as P

ASKER_PROJ_NUM = 16
KEY_VALUE_HEADS = 2
DELAY = 256
FLAG_ROWS = 16
LOG2E = math.log2(math.e)
MESH = pl.DeviceIdType.MESH


def kernel(
    n,
    head_devices,
    q_hbm,
    kc_hbm,
    ks_hbm,
    vc_hbm,
    vs_hbm,
    ev_hbm,
    of_hbm,
    go_hbm,
    ln_hbm,
    dq_ref,
    dk_ref,
    dv_ref,
    kv,
    part,
    core_in,
    y_in,
    z_in,
    y_out,
    z_out,
    q_rows,
    g_rows,
    q_cols,
    g_cols,
    norm,
    delta,
    dq_acc,
    group_sum,
    head_out,
    head_in,
    kz_send,
    kz_recv,
    ky_send,
    ky_recv,
    kc_send,
    kc_recv,
    rc_send,
    rc_recv,
    ry_send,
    ry_recv,
    rz_send,
    rz_recv,
    gs_send,
    gs_recv,
    h_send,
    h_recv,
    q_ref,
    kc_ref,
    ks_ref,
    vc_ref,
    vs_ref,
    ev_ref,
    of_ref,
    go_ref,
    ln_ref,
    in_sems,
):
    tokens, _ = q_ref.shape
    width = kc_ref.shape[1]
    heads = ln_ref.shape[0]
    half = tokens // 2
    zs = n // 4
    low_rows = 2 * half + FLAG_ROWS
    all_rows = 4 * half + FLAG_ROWS
    per_group = head_devices // KEY_VALUE_HEADS
    scale = width ** (-0.5)

    me = lax.axis_index("ctx")
    hd = lax.axis_index("head")
    c = lax.rem(me, 2)
    y = lax.rem(me // 2, 2)
    z = me // 4
    group = hd // per_group
    member = lax.rem(hd, per_group)

    def at(zi, yi, ci):
        return (zi * 4 + yi * 2 + ci, hd)

    core_peer = at(z, y, 1 - c)
    y_peer = at(z, 1 - y, c)
    other_group = (me, lax.rem(hd + per_group, head_devices))

    def turn(s):
        if zs & (zs - 1):
            return lax.rem(z + s, zs)
        out = 0
        bit = 1
        while bit < zs:
            out = out + lax.rem(z // bit + s // bit, 2) * bit
            bit *= 2
        return out

    barrier = pltpu.get_barrier_semaphore()
    pl.semaphore_signal(barrier, inc=1, device_id=core_peer, device_id_type=MESH)
    pl.semaphore_signal(barrier, inc=1, device_id=y_peer, device_id_type=MESH)
    pl.semaphore_signal(barrier, inc=1, device_id=other_group, device_id_type=MESH)
    for s in range(1, zs):
        pl.semaphore_signal(
            barrier, inc=1, device_id=at(turn(s), y, c), device_id_type=MESH
        )
    for s in range(1, per_group):
        pl.semaphore_signal(
            barrier,
            inc=1,
            device_id=(me, group * per_group + lax.rem(member + s, per_group)),
            device_id_type=MESH,
        )

    kv_loads = [
        pltpu.make_async_copy(src, dst, in_sems.at[i])
        for i, (src, dst) in enumerate(
            [
                (ks_hbm, ks_ref),
                (kc_hbm.at[group], kc_ref),
                (vs_hbm, vs_ref),
                (vc_hbm.at[group], vc_ref),
                (ev_hbm, ev_ref),
            ]
        )
    ]
    query_loads = [
        pltpu.make_async_copy(src, dst, in_sems.at[len(kv_loads) + i])
        for i, (src, dst) in enumerate(
            [(q_hbm, q_ref), (go_hbm, go_ref), (of_hbm, of_ref), (ln_hbm, ln_ref)]
        )
    ]
    for load in kv_loads + query_loads:
        load.start()
    for load in kv_loads:
        load.wait()

    def column(row):
        return jnp.transpose(jnp.broadcast_to(row, (tokens, tokens)))

    key_col = column(ks_ref[pl.ds(group, 1), :])
    value_col = column(vs_ref[pl.ds(group, 1), :])
    keys = (kc_ref[...].astype(jnp.float32) * key_col).astype(jnp.bfloat16)
    values = (vc_ref[...].astype(jnp.float32) * value_col).astype(jnp.bfloat16)
    flags = ev_ref[pl.ds(group, 1), :].astype(jnp.float32)
    own = kv.at[z, y, c]
    own[0:half, :] = keys[0:half]
    own[half : 2 * half, :] = values[0:half]
    own[2 * half : low_rows, :] = jnp.broadcast_to(flags, (FLAG_ROWS, tokens)).astype(
        jnp.bfloat16
    )
    own[low_rows : low_rows + half, :] = keys[half:]
    own[low_rows + half :, :] = values[half:]

    def prepare(side):
        tok = slice(side * half, (side + 1) * half)

        def by_head(ref):
            return jnp.concatenate(
                [ref[tok, h * width : (h + 1) * width] for h in range(heads)], axis=0
            )

        q = by_head(q_ref)
        g = by_head(go_ref)
        q_rows[side] = q
        g_rows[side] = g
        q_cols[side] = jnp.transpose(q)
        g_t = jnp.transpose(g)
        g_cols[side] = g_t
        o_t = jnp.transpose(by_head(of_ref))
        delta[side] = jnp.sum(
            g_t.astype(jnp.float32) * o_t.astype(jnp.float32), axis=0, keepdims=True
        )
        norm[side] = (
            jnp.concatenate([ln_ref[h : h + 1, tok] for h in range(heads)], axis=1)
            * LOG2E
        )
        dq_acc[side] = jnp.zeros(dq_acc.shape[1:], jnp.float32)

    pl.semaphore_wait(barrier, 3 + (zs - 1) + (per_group - 1))

    def sized(whole, f, full, low):
        @pl.when(whole)
        def _():
            f(pl.ds(0, full))

        @pl.when(jnp.logical_not(whole))
        def _():
            f(pl.ds(0, low))

    def kz_copy(src_z, dst_z, rows):
        return pltpu.make_async_remote_copy(
            src_ref=kv.at[z, y, c, rows],
            dst_ref=kv.at[src_z, y, c, rows],
            send_sem=kz_send.at[dst_z],
            recv_sem=kz_recv.at[src_z],
            device_id=at(dst_z, y, c),
            device_id_type=MESH,
        )

    def ky_copy(zi, yi, rows):
        ref = kv.at[zi, yi, c, rows]
        return pltpu.make_async_remote_copy(
            src_ref=ref,
            dst_ref=ref,
            send_sem=ky_send.at[zi],
            recv_sem=ky_recv.at[zi],
            device_id=y_peer,
            device_id_type=MESH,
        )

    def kc_copy(zi, ci, rows):
        ref = kv.at[zi, :, ci, rows]
        return pltpu.make_async_remote_copy(
            src_ref=ref,
            dst_ref=ref,
            send_sem=kc_send.at[zi],
            recv_sem=kc_recv.at[zi],
            device_id=core_peer,
            device_id_type=MESH,
        )

    def send_z(s, carry):
        zi = turn(s)
        sized(z >= zi, lambda rows: kz_copy(z, zi, rows).start(), all_rows, low_rows)
        return carry

    lax.fori_loop(1, zs, send_z, 0)

    def forward_y(s):
        zi = turn(s)

        def go(rows):
            @pl.when(zi != z)
            def _():
                kz_copy(zi, zi, rows).wait_recv()

            ky_copy(zi, y, rows).start()

        sized(zi >= z, go, all_rows, low_rows)

    def forward_c(s):
        zi = turn(s)

        def go(rows):
            ky_copy(zi, 1 - y, rows).wait_recv()
            kc_copy(zi, c, rows).start()

        sized(zi >= z, go, all_rows, low_rows)

    def ready(s):
        zi = turn(s)
        sized(
            zi >= z,
            lambda rows: kc_copy(zi, 1 - c, rows).wait_recv(),
            all_rows,
            low_rows,
        )

    forward_y(0)
    for load in query_loads:
        load.wait()
    prepare(1)
    forward_c(0)
    forward_y(1)
    prepare(0)

    chunk = 4 * half
    lanes = 2 * half
    copies = heads * half // lanes
    row = lax.broadcasted_iota(jnp.int32, (chunk, lanes), 0)
    lane = lax.broadcasted_iota(jnp.int32, (chunk, lanes), 1)
    row_block = row // half
    row_in = lax.rem(row, half)
    lane_in = lax.rem(lane, half)

    def terms(k, v, k_t, key_pos, limit, side):
        block = me if side == 0 else 2 * n - 1 - me
        distance = block * half + lane_in - key_pos
        visible = (distance >= 0) & (distance < limit)
        bias = jnp.where(visible, 0.0, -1e30)
        bias = jnp.concatenate([bias] * copies, axis=1)
        scores = jnp.dot(k, q_cols[side], preferred_element_type=jnp.float32)
        weights = jnp.exp2(scores * (scale * LOG2E) - norm[side] + bias)
        dweights = jnp.dot(v, g_cols[side], preferred_element_type=jnp.float32)
        dscores = (scale * weights * (dweights - delta[side])).astype(jnp.bfloat16)
        weights = weights.astype(jnp.bfloat16)
        dq_acc[side] += jnp.dot(k_t, dscores, preferred_element_type=jnp.float32)
        dk = jnp.dot(dscores, q_rows[side], preferred_element_type=jnp.float32)
        dv = jnp.dot(weights, g_rows[side], preferred_element_type=jnp.float32)
        return dk.reshape(2, 2, half, width), dv.reshape(2, 2, half, width)

    def limits(zi, first):
        cols = [
            column(kv[zi, yi, ci, 2 * half : 2 * half + FLAG_ROWS, :].astype(jnp.float32)[0:1])[
                first : first + half
            ]
            for yi in range(2)
            for ci in range(2)
        ]
        evicted = jnp.concatenate(cols, axis=0)
        return jnp.where(evicted == 0.0, 2 * n * half, DELAY)

    def compute(s):
        zi = turn(s)
        k = kv[zi, :, :, 0:half, :].reshape(chunk, width)
        v = kv[zi, :, :, half : 2 * half, :].reshape(chunk, width)
        k_t = jnp.transpose(k)
        key_pos = (zi * 4 + row_block) * half + row_in
        limit = limits(zi, 0)
        dk, dv = terms(k, v, k_t, key_pos, limit, 1)
        part[zi, :, :, 0:half, :] = dk
        part[zi, :, :, half : 2 * half, :] = dv

        @pl.when(zi <= z)
        def _():
            dk, dv = terms(k, v, k_t, key_pos, limit, 0)
            part[zi, :, :, 0:half, :] += dk
            part[zi, :, :, half : 2 * half, :] += dv

        @pl.when(zi >= z)
        def _():
            k = kv[zi, :, :, low_rows : low_rows + half, :].reshape(chunk, width)
            v = kv[zi, :, :, low_rows + half :, :].reshape(chunk, width)
            key_pos = (2 * n - 1 - zi * 4 - row_block) * half + row_in
            dk, dv = terms(k, v, jnp.transpose(k), key_pos, limits(zi, half), 1)
            part[zi, :, :, 2 * half : 3 * half, :] = dk
            part[zi, :, :, 3 * half :, :] = dv

    def rc_copy(zi, rows):
        return pltpu.make_async_remote_copy(
            src_ref=part.at[zi, :, 1 - c, rows],
            dst_ref=core_in.at[zi, :, rows],
            send_sem=rc_send.at[zi],
            recv_sem=rc_recv.at[zi],
            device_id=core_peer,
            device_id_type=MESH,
        )

    def ry_copy(zi, rows):
        return pltpu.make_async_remote_copy(
            src_ref=y_out.at[zi, rows],
            dst_ref=y_in.at[zi, rows],
            send_sem=ry_send.at[zi],
            recv_sem=ry_recv.at[zi],
            device_id=y_peer,
            device_id_type=MESH,
        )

    def rz_copy(src_z, dst_z, rows):
        return pltpu.make_async_remote_copy(
            src_ref=z_out.at[dst_z, rows],
            dst_ref=z_in.at[src_z, rows],
            send_sem=rz_send.at[dst_z],
            recv_sem=rz_recv.at[src_z],
            device_id=at(dst_z, y, c),
            device_id_type=MESH,
        )

    def reduce_c(s):
        zi = turn(s)
        sized(zi >= z, lambda rows: rc_copy(zi, rows).start(), 4 * half, 2 * half)

    def reduce_y(s):
        zi = turn(s)

        def go(rows):
            rc_copy(zi, rows).wait_recv()
            for yi in range(2):
                part[zi, yi, c, rows, :] += core_in[zi, yi, rows, :]
            y_out[zi, rows, :] = part[zi, 1 - y, c, rows, :].astype(jnp.bfloat16)
            ry_copy(zi, rows).start()

        sized(zi >= z, go, 4 * half, 2 * half)

    def reduce_z(s):
        zi = turn(s)

        def go(rows):
            ry_copy(zi, rows).wait_recv()
            part[zi, y, c, rows, :] += y_in[zi, rows, :].astype(jnp.float32)

            @pl.when(zi != z)
            def _():
                z_out[zi, rows, :] = part[zi, y, c, rows, :].astype(jnp.bfloat16)
                rz_copy(z, zi, rows).start()

        sized(zi >= z, go, 4 * half, 2 * half)

    def when(cond, f, s):
        @pl.when(cond)
        def _():
            f(s)

    def step(s, carry):
        when(s + 2 < zs, forward_y, s + 2)
        when(s + 1 < zs, forward_c, s + 1)
        ready(s)
        compute(s)
        reduce_c(s)
        when(s >= 1, reduce_y, s - 1)
        when(s >= 2, reduce_z, s - 2)
        return carry

    lax.fori_loop(0, zs, step, 0)
    reduce_y(zs - 1)
    if zs >= 2:
        reduce_z(zs - 2)
    reduce_z(zs - 1)

    for side in range(2):
        dq = jnp.transpose(dq_acc[side]).astype(jnp.bfloat16)
        for h in range(heads):
            dq_ref[side * half : (side + 1) * half, h * width : (h + 1) * width] = dq[
                h * half : (h + 1) * half
            ]

    def collect(s, carry):
        zi = turn(s)

        def go(rows):
            rz_copy(zi, zi, rows).wait_recv()
            part[z, y, c, rows, :] += z_in[zi, rows, :].astype(jnp.float32)

        sized(z >= zi, go, 4 * half, 2 * half)
        return carry

    lax.fori_loop(1, zs, collect, 0)

    total = part[z, y, c]
    if per_group > 1:
        group_sum[member] = total

        def gs_copy(src, s):
            return pltpu.make_async_remote_copy(
                src_ref=group_sum.at[member],
                dst_ref=group_sum.at[src],
                send_sem=gs_send.at[s],
                recv_sem=gs_recv.at[src],
                device_id=(me, group * per_group + lax.rem(member + s, per_group)),
                device_id_type=MESH,
            )

        for s in range(1, per_group):
            gs_copy(member, s).start()
        for s in range(1, per_group):
            gs_copy(lax.rem(member + s, per_group), s).wait_recv()
        for s in range(1, per_group):
            gs_copy(member, s).wait_send()
        total = group_sum[0]
        for s in range(1, per_group):
            total = total + group_sum[s]

    head_out[...] = total.astype(jnp.bfloat16)
    h_copy = pltpu.make_async_remote_copy(
        src_ref=head_out,
        dst_ref=head_in,
        send_sem=h_send,
        recv_sem=h_recv,
        device_id=other_group,
        device_id_type=MESH,
    )
    h_copy.start()

    def put(index, block):
        dk_ref[index, 0:half, :] = block[0:half, :]
        dv_ref[index, 0:half, :] = block[half : 2 * half, :]
        dk_ref[index, half:, :] = block[2 * half : 3 * half, :]
        dv_ref[index, half:, :] = block[3 * half :, :]

    put(group, head_out)

    def sent(s, carry):
        zi = turn(s)

        def own_z(rows):
            kz_copy(z, zi, rows).wait_send()

        def kept(rows):
            ky_copy(zi, y, rows).wait_send()
            kc_copy(zi, c, rows).wait_send()

        def summed(rows):
            rc_copy(zi, rows).wait_send()
            ry_copy(zi, rows).wait_send()

            @pl.when(zi != z)
            def _():
                rz_copy(z, zi, rows).wait_send()

        @pl.when(zi != z)
        def _():
            sized(z >= zi, own_z, all_rows, low_rows)

        sized(zi >= z, kept, all_rows, low_rows)
        sized(zi >= z, summed, 4 * half, 2 * half)
        return carry

    lax.fori_loop(0, zs, sent, 0)
    h_copy.wait()
    put(1 - group, head_in)


def local(
    queries,
    key_codes,
    key_scale,
    value_codes,
    value_scale,
    evict_flags,
    out_forward,
    grad_output,
    log_norm,
):
    n = lax.axis_size("ctx")
    head_devices = lax.axis_size("head")
    per_group = head_devices // KEY_VALUE_HEADS
    tokens = queries.shape[0]
    heads = log_norm.shape[0]
    width = key_codes.shape[2]
    half = tokens // 2
    zs = n // 4
    side_rows = heads * half
    f32, bf16 = jnp.float32, jnp.bfloat16
    vmem = pl.BlockSpec(memory_space=pltpu.VMEM)
    dma = pltpu.SemaphoreType.DMA
    return pl.pallas_call(
        functools.partial(kernel, n, head_devices),
        out_shape=(
            jax.ShapeDtypeStruct(queries.shape, bf16),
            jax.ShapeDtypeStruct(key_codes.shape, bf16),
            jax.ShapeDtypeStruct(value_codes.shape, bf16),
        ),
        in_specs=[pl.BlockSpec(memory_space=pltpu.HBM)] * 9,
        out_specs=(vmem, vmem, vmem),
        scratch_shapes=[
            pltpu.VMEM((zs, 2, 2, 4 * half + FLAG_ROWS, width), bf16),
            pltpu.VMEM((zs, 2, 2, 4 * half, width), f32),
            pltpu.VMEM((zs, 2, 4 * half, width), f32),
            pltpu.VMEM((zs, 4 * half, width), bf16),
            pltpu.VMEM((zs, 4 * half, width), bf16),
            pltpu.VMEM((zs, 4 * half, width), bf16),
            pltpu.VMEM((zs, 4 * half, width), bf16),
            pltpu.VMEM((2, side_rows, width), bf16),
            pltpu.VMEM((2, side_rows, width), bf16),
            pltpu.VMEM((2, width, side_rows), bf16),
            pltpu.VMEM((2, width, side_rows), bf16),
            pltpu.VMEM((2, 1, side_rows), f32),
            pltpu.VMEM((2, 1, side_rows), f32),
            pltpu.VMEM((2, width, side_rows), f32),
            pltpu.VMEM((per_group, 4 * half, width), f32),
            pltpu.VMEM((4 * half, width), bf16),
            pltpu.VMEM((4 * half, width), bf16),
        ]
        + [dma((zs,))] * 12
        + [dma((per_group,))] * 2
        + [dma] * 2
        + [
            pltpu.VMEM(queries.shape, bf16),
            pltpu.VMEM(key_codes.shape[1:], bf16),
            pltpu.VMEM(key_scale.shape, f32),
            pltpu.VMEM(value_codes.shape[1:], bf16),
            pltpu.VMEM(value_scale.shape, f32),
            pltpu.VMEM(evict_flags.shape, jnp.int32),
            pltpu.VMEM(out_forward.shape, bf16),
            pltpu.VMEM(grad_output.shape, bf16),
            pltpu.VMEM(log_norm.shape, f32),
            dma((9,)),
        ],
        compiler_params=pltpu.CompilerParams(
            collective_id=0, has_side_effects=True, vmem_limit_bytes=48 * 2**20
        ),
    )(
        queries,
        key_codes,
        key_scale,
        value_codes,
        value_scale,
        evict_flags,
        out_forward,
        grad_output,
        log_norm,
    )


def solution(mesh):
    in_specs = (
        P("ctx", "head"),
        P(None, "ctx", None),
        P(None, "ctx"),
        P(None, "ctx", None),
        P(None, "ctx"),
        P(None, "ctx"),
        P("ctx", "head"),
        P("ctx", "head"),
        P("head", "ctx"),
    )
    out_specs = (P("ctx", "head"), P(None, "ctx", None), P(None, "ctx", None))
    return jax.shard_map(local, mesh=mesh, in_specs=in_specs, out_specs=out_specs, check_vma=False)
```

```python
import functools
import math

import jax
import jax.numpy as jnp
from jax import lax
from jax.experimental import pallas as pl
from jax.experimental.pallas import tpu as pltpu
from jax.sharding import PartitionSpec as P

ASKER_PROJ_NUM = 16
KEY_VALUE_HEADS = 2
DELAY = 256
FLAG_ROWS = 16
LOG2E = math.log2(math.e)
MESH = pl.DeviceIdType.MESH


def kernel(
    n,
    head_devices,
    q_hbm,
    kc_hbm,
    ks_hbm,
    vc_hbm,
    vs_hbm,
    ev_hbm,
    of_hbm,
    go_hbm,
    ln_hbm,
    dq_ref,
    dk_ref,
    dv_ref,
    kv,
    part,
    core_in,
    y_in,
    z_in,
    y_out,
    z_out,
    q_rows,
    g_rows,
    q_cols,
    g_cols,
    norm,
    delta,
    dq_acc,
    group_sum,
    head_out,
    head_in,
    kz_send,
    kz_recv,
    ky_send,
    ky_recv,
    kc_send,
    kc_recv,
    rc_send,
    rc_recv,
    ry_send,
    ry_recv,
    rz_send,
    rz_recv,
    gs_send,
    gs_recv,
    h_send,
    h_recv,
    q_ref,
    kc_ref,
    ks_ref,
    vc_ref,
    vs_ref,
    ev_ref,
    of_ref,
    go_ref,
    ln_ref,
    in_sems,
):
    tokens, _ = q_ref.shape
    width = kc_ref.shape[1]
    heads = ln_ref.shape[0]
    half = tokens // 2
    zs = n // 4
    low_rows = 2 * half + FLAG_ROWS
    all_rows = 4 * half + FLAG_ROWS
    per_group = head_devices // KEY_VALUE_HEADS
    scale = width ** (-0.5)

    me = lax.axis_index("ctx")
    hd = lax.axis_index("head")
    c = lax.rem(me, 2)
    y = lax.rem(me // 2, 2)
    z = me // 4
    group = hd // per_group
    member = lax.rem(hd, per_group)

    def at(zi, yi, ci):
        return (zi * 4 + yi * 2 + ci, hd)

    core_peer = at(z, y, 1 - c)
    y_peer = at(z, 1 - y, c)
    other_group = (me, lax.rem(hd + per_group, head_devices))

    def turn(s):
        if zs & (zs - 1):
            return lax.rem(z + s, zs)
        out = 0
        bit = 1
        while bit < zs:
            out = out + lax.rem(z // bit + s // bit, 2) * bit
            bit *= 2
        return out

    barrier = pltpu.get_barrier_semaphore()
    pl.semaphore_signal(barrier, inc=1, device_id=core_peer, device_id_type=MESH)
    pl.semaphore_signal(barrier, inc=1, device_id=y_peer, device_id_type=MESH)
    pl.semaphore_signal(barrier, inc=1, device_id=other_group, device_id_type=MESH)
    for s in range(1, zs):
        pl.semaphore_signal(
            barrier, inc=1, device_id=at(turn(s), y, c), device_id_type=MESH
        )
    for s in range(1, per_group):
        pl.semaphore_signal(
            barrier,
            inc=1,
            device_id=(me, group * per_group + lax.rem(member + s, per_group)),
            device_id_type=MESH,
        )

    kv_loads = [
        pltpu.make_async_copy(src, dst, in_sems.at[i])
        for i, (src, dst) in enumerate(
            [
                (ks_hbm, ks_ref),
                (kc_hbm.at[group], kc_ref),
                (vs_hbm, vs_ref),
                (vc_hbm.at[group], vc_ref),
                (ev_hbm, ev_ref),
            ]
        )
    ]
    query_loads = [
        pltpu.make_async_copy(src, dst, in_sems.at[len(kv_loads) + i])
        for i, (src, dst) in enumerate(
            [(q_hbm, q_ref), (go_hbm, go_ref), (of_hbm, of_ref), (ln_hbm, ln_ref)]
        )
    ]
    for load in kv_loads + query_loads:
        load.start()
    for load in kv_loads:
        load.wait()

    def column(row):
        return jnp.transpose(jnp.broadcast_to(row, (tokens, tokens)))

    key_col = column(ks_ref[pl.ds(group, 1), :])
    value_col = column(vs_ref[pl.ds(group, 1), :])
    keys = (kc_ref[...].astype(jnp.float32) * key_col).astype(jnp.bfloat16)
    values = (vc_ref[...].astype(jnp.float32) * value_col).astype(jnp.bfloat16)
    flags = ev_ref[pl.ds(group, 1), :].astype(jnp.float32)
    own = kv.at[z, y, c]
    own[0:half, :] = keys[0:half]
    own[half : 2 * half, :] = values[0:half]
    own[2 * half : low_rows, :] = jnp.broadcast_to(flags, (FLAG_ROWS, tokens)).astype(
        jnp.bfloat16
    )
    own[low_rows : low_rows + half, :] = keys[half:]
    own[low_rows + half :, :] = values[half:]

    def prepare(side):
        tok = slice(side * half, (side + 1) * half)

        def by_head(ref):
            return jnp.concatenate(
                [ref[tok, h * width : (h + 1) * width] for h in range(heads)], axis=0
            )

        q = by_head(q_ref)
        g = by_head(go_ref)
        q_rows[side] = q
        g_rows[side] = g
        q_cols[side] = jnp.transpose(q)
        g_t = jnp.transpose(g)
        g_cols[side] = g_t
        o_t = jnp.transpose(by_head(of_ref))
        delta[side] = jnp.sum(
            g_t.astype(jnp.float32) * o_t.astype(jnp.float32), axis=0, keepdims=True
        )
        norm[side] = (
            jnp.concatenate([ln_ref[h : h + 1, tok] for h in range(heads)], axis=1)
            * LOG2E
        )
        dq_acc[side] = jnp.zeros(dq_acc.shape[1:], jnp.float32)

    pl.semaphore_wait(barrier, 3 + (zs - 1) + (per_group - 1))

    def sized(whole, f, full, low):
        @pl.when(whole)
        def _():
            f(pl.ds(0, full))

        @pl.when(jnp.logical_not(whole))
        def _():
            f(pl.ds(0, low))

    def kz_copy(src_z, dst_z, rows):
        return pltpu.make_async_remote_copy(
            src_ref=kv.at[z, y, c, rows],
            dst_ref=kv.at[src_z, y, c, rows],
            send_sem=kz_send.at[dst_z],
            recv_sem=kz_recv.at[src_z],
            device_id=at(dst_z, y, c),
            device_id_type=MESH,
        )

    def ky_copy(zi, yi, rows):
        ref = kv.at[zi, yi, c, rows]
        return pltpu.make_async_remote_copy(
            src_ref=ref,
            dst_ref=ref,
            send_sem=ky_send.at[zi],
            recv_sem=ky_recv.at[zi],
            device_id=y_peer,
            device_id_type=MESH,
        )

    def kc_copy(zi, ci, rows):
        ref = kv.at[zi, :, ci, rows]
        return pltpu.make_async_remote_copy(
            src_ref=ref,
            dst_ref=ref,
            send_sem=kc_send.at[zi],
            recv_sem=kc_recv.at[zi],
            device_id=core_peer,
            device_id_type=MESH,
        )

    def send_z(s, carry):
        zi = turn(s)
        sized(z >= zi, lambda rows: kz_copy(z, zi, rows).start(), all_rows, low_rows)
        return carry

    lax.fori_loop(1, zs, send_z, 0)

    def forward_y(s):
        zi = turn(s)

        def go(rows):
            @pl.when(zi != z)
            def _():
                kz_copy(zi, zi, rows).wait_recv()

            ky_copy(zi, y, rows).start()

        sized(zi >= z, go, all_rows, low_rows)

    def forward_c(s):
        zi = turn(s)

        def go(rows):
            ky_copy(zi, 1 - y, rows).wait_recv()
            kc_copy(zi, c, rows).start()

        sized(zi >= z, go, all_rows, low_rows)

    def ready(s):
        zi = turn(s)
        sized(
            zi >= z,
            lambda rows: kc_copy(zi, 1 - c, rows).wait_recv(),
            all_rows,
            low_rows,
        )

    forward_y(0)
    for load in query_loads:
        load.wait()
    prepare(1)
    forward_c(0)
    forward_y(1)
    prepare(0)

    chunk = 4 * half
    lanes = 2 * half
    copies = heads * half // lanes
    row = lax.broadcasted_iota(jnp.int32, (chunk, lanes), 0)
    lane = lax.broadcasted_iota(jnp.int32, (chunk, lanes), 1)
    row_block = row // half
    row_in = lax.rem(row, half)
    lane_in = lax.rem(lane, half)

    def terms(k, v, k_t, key_pos, limit, side):
        block = me if side == 0 else 2 * n - 1 - me
        distance = block * half + lane_in - key_pos
        visible = (distance >= 0) & (distance < limit)
        bias = jnp.where(visible, 0.0, -1e30)
        bias = jnp.concatenate([bias] * copies, axis=1)
        scores = jnp.dot(k, q_cols[side], preferred_element_type=jnp.float32)
        weights = jnp.exp2(scores * (scale * LOG2E) - norm[side] + bias)
        dweights = jnp.dot(v, g_cols[side], preferred_element_type=jnp.float32)
        dscores = (scale * weights * (dweights - delta[side])).astype(jnp.bfloat16)
        weights = weights.astype(jnp.bfloat16)
        dq_acc[side] += jnp.dot(k_t, dscores, preferred_element_type=jnp.float32)
        dk = jnp.dot(dscores, q_rows[side], preferred_element_type=jnp.float32)
        dv = jnp.dot(weights, g_rows[side], preferred_element_type=jnp.float32)
        return dk.reshape(2, 2, half, width), dv.reshape(2, 2, half, width)

    def limits(zi, first):
        cols = [
            column(kv[zi, yi, ci, 2 * half : 2 * half + FLAG_ROWS, :].astype(jnp.float32)[0:1])[
                first : first + half
            ]
            for yi in range(2)
            for ci in range(2)
        ]
        evicted = jnp.concatenate(cols, axis=0)
        return jnp.where(evicted == 0.0, 2 * n * half, DELAY)

    def compute_high(zi):
        k = kv[zi, :, :, low_rows : low_rows + half, :].reshape(chunk, width)
        v = kv[zi, :, :, low_rows + half :, :].reshape(chunk, width)
        key_pos = (2 * n - 1 - zi * 4 - row_block) * half + row_in
        dk, dv = terms(k, v, jnp.transpose(k), key_pos, limits(zi, half), 1)
        part[zi, :, :, 2 * half : 3 * half, :] = dk
        part[zi, :, :, 3 * half :, :] = dv

    def compute(s):
        zi = turn(s)
        k = kv[zi, :, :, 0:half, :].reshape(chunk, width)
        v = kv[zi, :, :, half : 2 * half, :].reshape(chunk, width)
        k_t = jnp.transpose(k)
        key_pos = (zi * 4 + row_block) * half + row_in
        limit = limits(zi, 0)
        dk, dv = terms(k, v, k_t, key_pos, limit, 1)
        part[zi, :, :, 0:half, :] = dk
        part[zi, :, :, half : 2 * half, :] = dv

        @pl.when(zi <= z)
        def _():
            dk, dv = terms(k, v, k_t, key_pos, limit, 0)
            part[zi, :, :, 0:half, :] += dk
            part[zi, :, :, half : 2 * half, :] += dv

        @pl.when(zi > z)
        def _():
            compute_high(zi)

    def rc_copy(zi, rows):
        return pltpu.make_async_remote_copy(
            src_ref=part.at[zi, :, 1 - c, rows],
            dst_ref=core_in.at[zi, :, rows],
            send_sem=rc_send.at[zi],
            recv_sem=rc_recv.at[zi],
            device_id=core_peer,
            device_id_type=MESH,
        )

    def ry_copy(zi, rows):
        return pltpu.make_async_remote_copy(
            src_ref=y_out.at[zi, rows],
            dst_ref=y_in.at[zi, rows],
            send_sem=ry_send.at[zi],
            recv_sem=ry_recv.at[zi],
            device_id=y_peer,
            device_id_type=MESH,
        )

    def rz_copy(src_z, dst_z, rows):
        return pltpu.make_async_remote_copy(
            src_ref=z_out.at[dst_z, rows],
            dst_ref=z_in.at[src_z, rows],
            send_sem=rz_send.at[dst_z],
            recv_sem=rz_recv.at[src_z],
            device_id=at(dst_z, y, c),
            device_id_type=MESH,
        )

    def reduce_c(s):
        zi = turn(s)
        sized(zi >= z, lambda rows: rc_copy(zi, rows).start(), 4 * half, 2 * half)

    def reduce_y(s):
        zi = turn(s)

        def go(rows):
            rc_copy(zi, rows).wait_recv()
            for yi in range(2):
                part[zi, yi, c, rows, :] += core_in[zi, yi, rows, :]
            y_out[zi, rows, :] = part[zi, 1 - y, c, rows, :].astype(jnp.bfloat16)
            ry_copy(zi, rows).start()

        sized(zi >= z, go, 4 * half, 2 * half)

    def reduce_z(s):
        zi = turn(s)

        def go(rows):
            ry_copy(zi, rows).wait_recv()
            part[zi, y, c, rows, :] += y_in[zi, rows, :].astype(jnp.float32)

            @pl.when(zi != z)
            def _():
                z_out[zi, rows, :] = part[zi, y, c, rows, :].astype(jnp.bfloat16)
                rz_copy(z, zi, rows).start()

        sized(zi >= z, go, 4 * half, 2 * half)

    def when(cond, f, s):
        @pl.when(cond)
        def _():
            f(s)

    def step(s, carry):
        when(s + 2 < zs, forward_y, s + 2)
        when(s + 1 < zs, forward_c, s + 1)
        ready(s)
        compute(s)
        when(s >= 1, reduce_c, s)
        when(s >= 2, reduce_y, s - 1)
        when(s >= 3, reduce_z, s - 2)
        return carry

    lax.fori_loop(0, zs, step, 0)
    compute_high(z)
    reduce_c(0)
    if zs >= 2:
        reduce_y(zs - 1)
    if zs >= 3:
        reduce_z(zs - 2)
    reduce_y(0)
    if zs >= 2:
        reduce_z(zs - 1)

    for side in range(2):
        dq = jnp.transpose(dq_acc[side]).astype(jnp.bfloat16)
        for h in range(heads):
            dq_ref[side * half : (side + 1) * half, h * width : (h + 1) * width] = dq[
                h * half : (h + 1) * half
            ]

    reduce_z(0)

    def collect(s, carry):
        zi = turn(s)

        def go(rows):
            rz_copy(zi, zi, rows).wait_recv()
            part[z, y, c, rows, :] += z_in[zi, rows, :].astype(jnp.float32)

        sized(z >= zi, go, 4 * half, 2 * half)
        return carry

    lax.fori_loop(1, zs, collect, 0)

    total = part[z, y, c]
    if per_group > 1:
        group_sum[member] = total

        def gs_copy(src, s):
            return pltpu.make_async_remote_copy(
                src_ref=group_sum.at[member],
                dst_ref=group_sum.at[src],
                send_sem=gs_send.at[s],
                recv_sem=gs_recv.at[src],
                device_id=(me, group * per_group + lax.rem(member + s, per_group)),
                device_id_type=MESH,
            )

        for s in range(1, per_group):
            gs_copy(member, s).start()
        for s in range(1, per_group):
            gs_copy(lax.rem(member + s, per_group), s).wait_recv()
        for s in range(1, per_group):
            gs_copy(member, s).wait_send()
        total = group_sum[0]
        for s in range(1, per_group):
            total = total + group_sum[s]

    head_out[...] = total.astype(jnp.bfloat16)
    h_copy = pltpu.make_async_remote_copy(
        src_ref=head_out,
        dst_ref=head_in,
        send_sem=h_send,
        recv_sem=h_recv,
        device_id=other_group,
        device_id_type=MESH,
    )
    h_copy.start()

    def put(index, block):
        dk_ref[index, 0:half, :] = block[0:half, :]
        dv_ref[index, 0:half, :] = block[half : 2 * half, :]
        dk_ref[index, half:, :] = block[2 * half : 3 * half, :]
        dv_ref[index, half:, :] = block[3 * half :, :]

    put(group, head_out)

    def sent(s, carry):
        zi = turn(s)

        def own_z(rows):
            kz_copy(z, zi, rows).wait_send()

        def kept(rows):
            ky_copy(zi, y, rows).wait_send()
            kc_copy(zi, c, rows).wait_send()

        def summed(rows):
            rc_copy(zi, rows).wait_send()
            ry_copy(zi, rows).wait_send()

            @pl.when(zi != z)
            def _():
                rz_copy(z, zi, rows).wait_send()

        @pl.when(zi != z)
        def _():
            sized(z >= zi, own_z, all_rows, low_rows)

        sized(zi >= z, kept, all_rows, low_rows)
        sized(zi >= z, summed, 4 * half, 2 * half)
        return carry

    lax.fori_loop(0, zs, sent, 0)
    h_copy.wait()
    put(1 - group, head_in)


def place(dq, dk, dv, dq_out, dk_out, dv_out, dq_vmem, dk_vmem, dv_vmem, in_sems, out_sems):
    held = (dq_vmem, dk_vmem, dv_vmem)
    loads = [
        pltpu.make_async_copy(src, dst, in_sems.at[i])
        for i, (src, dst) in enumerate(zip((dq, dk, dv), held))
    ]
    stores = [
        pltpu.make_async_copy(src, dst, out_sems.at[i])
        for i, (src, dst) in enumerate(zip(held, (dq_out, dk_out, dv_out)))
    ]
    for load in loads:
        load.start()
    for load, store in zip(loads, stores):
        load.wait()
        store.start()
    for store in stores:
        store.wait()


def local(
    queries,
    key_codes,
    key_scale,
    value_codes,
    value_scale,
    evict_flags,
    out_forward,
    grad_output,
    log_norm,
):
    n = lax.axis_size("ctx")
    head_devices = lax.axis_size("head")
    per_group = head_devices // KEY_VALUE_HEADS
    tokens = queries.shape[0]
    heads = log_norm.shape[0]
    width = key_codes.shape[2]
    half = tokens // 2
    zs = n // 4
    side_rows = heads * half
    f32, bf16 = jnp.float32, jnp.bfloat16
    vmem = pl.BlockSpec(memory_space=pltpu.VMEM)
    dma = pltpu.SemaphoreType.DMA
    grads = pl.pallas_call(
        functools.partial(kernel, n, head_devices),
        out_shape=(
            jax.ShapeDtypeStruct(queries.shape, bf16),
            jax.ShapeDtypeStruct(key_codes.shape, bf16),
            jax.ShapeDtypeStruct(value_codes.shape, bf16),
        ),
        in_specs=[pl.BlockSpec(memory_space=pltpu.HBM)] * 9,
        out_specs=(vmem, vmem, vmem),
        scratch_shapes=[
            pltpu.VMEM((zs, 2, 2, 4 * half + FLAG_ROWS, width), bf16),
            pltpu.VMEM((zs, 2, 2, 4 * half, width), f32),
            pltpu.VMEM((zs, 2, 4 * half, width), f32),
            pltpu.VMEM((zs, 4 * half, width), bf16),
            pltpu.VMEM((zs, 4 * half, width), bf16),
            pltpu.VMEM((zs, 4 * half, width), bf16),
            pltpu.VMEM((zs, 4 * half, width), bf16),
            pltpu.VMEM((2, side_rows, width), bf16),
            pltpu.VMEM((2, side_rows, width), bf16),
            pltpu.VMEM((2, width, side_rows), bf16),
            pltpu.VMEM((2, width, side_rows), bf16),
            pltpu.VMEM((2, 1, side_rows), f32),
            pltpu.VMEM((2, 1, side_rows), f32),
            pltpu.VMEM((2, width, side_rows), f32),
            pltpu.VMEM((per_group, 4 * half, width), f32),
            pltpu.VMEM((4 * half, width), bf16),
            pltpu.VMEM((4 * half, width), bf16),
        ]
        + [dma((zs,))] * 12
        + [dma((per_group,))] * 2
        + [dma] * 2
        + [
            pltpu.VMEM(queries.shape, bf16),
            pltpu.VMEM(key_codes.shape[1:], bf16),
            pltpu.VMEM(key_scale.shape, f32),
            pltpu.VMEM(value_codes.shape[1:], bf16),
            pltpu.VMEM(value_scale.shape, f32),
            pltpu.VMEM(evict_flags.shape, jnp.int32),
            pltpu.VMEM(out_forward.shape, bf16),
            pltpu.VMEM(grad_output.shape, bf16),
            pltpu.VMEM(log_norm.shape, f32),
            dma((9,)),
        ],
        compiler_params=pltpu.CompilerParams(
            collective_id=0, has_side_effects=True, vmem_limit_bytes=62 * 2**20
        ),
    )(
        queries,
        key_codes,
        key_scale,
        value_codes,
        value_scale,
        evict_flags,
        out_forward,
        grad_output,
        log_norm,
    )
    anywhere = pl.BlockSpec(memory_space=pl.ANY)
    return pl.pallas_call(
        place,
        out_shape=tuple(jax.ShapeDtypeStruct(g.shape, g.dtype) for g in grads),
        in_specs=[anywhere] * 3,
        out_specs=(anywhere,) * 3,
        scratch_shapes=[pltpu.VMEM(g.shape, g.dtype) for g in grads] + [dma((3,))] * 2,
    )(*grads)


def solution(mesh):
    in_specs = (
        P("ctx", "head"),
        P(None, "ctx", None),
        P(None, "ctx"),
        P(None, "ctx", None),
        P(None, "ctx"),
        P(None, "ctx"),
        P("ctx", "head"),
        P("ctx", "head"),
        P("head", "ctx"),
    )
    out_specs = (P("ctx", "head"), P(None, "ctx", None), P(None, "ctx", None))
    return jax.shard_map(local, mesh=mesh, in_specs=in_specs, out_specs=out_specs, check_vma=False)
```
